32 devices in a mesh: row: 16 (over z, x, core), col: 2 (over y).
Axes of the slice: x: 2, y: 2, z: 4, core: 2. Of those that a mesh axis runs over, the one named last changes fastest.
Arguments:
- errors: bfloat16 [4096, 8192], P('col', 'row'), may hold values from -0.375 to 0.375
- inputs: bfloat16 [4096, 8192], P('row', 'col'), may hold values from -6 to 6
- weight: float32 [8192, 8192], P('row', 'col'), may hold values from -3 to 3
- weight_moment_one: bfloat16 [8192, 8192], P('row', 'col'), may hold values from -3 to 3
- weight_moment_two: bfloat16 [8192, 8192], P('row', 'col'), may hold values from 0.049804688 to 2
- feedback: float32 [2, 4096, 8192], P(None, 'row', 'col'), may hold values from -3 to 3
- feedback_moment_one: bfloat16 [2, 4096, 8192], P(None, 'row', 'col'), may hold values from -3 to 3
- feedback_moment_two: bfloat16 [2, 4096, 8192], P(None, 'row', 'col'), may hold values from 0.049804688 to 2
Outputs:
- new_weight: float32 [8192, 8192], P('row', 'col')
- new_weight_moment_one: bfloat16 [8192, 8192], P('row', 'col')
- new_weight_moment_two: bfloat16 [8192, 8192], P('row', 'col')
- weight_copy: bfloat16 [8192, 8192], P('row', 'col')
- new_feedback: float32 [2, 4096, 8192], P(None, 'row', 'col')
- new_feedback_moment_one: bfloat16 [2, 4096, 8192], P(None, 'row', 'col')
- new_feedback_moment_two: bfloat16 [2, 4096, 8192], P(None, 'row', 'col')
- feedback_copy: bfloat16 [2, 4096, 8192], P(None, 'row', 'col')
The draws below stay inside these ranges and needn't reach their ends.
All inputs are finite; a program needn't handle non-finite values.
Results may differ from the reference program's by a relative error of at most 0.001.
Values may be sent and summed in bfloat16 or wider, within the bound.
No kernel may reach another device: no remote copies, remote signals or barrier semaphores. Data moves between devices by JAX's collectives and lax.ppermute only.
A program may use at most 192 MiB of HBM per device.

```python
import math
import jax
import jax.numpy as jnp
from jax import lax

D = 8192
TOKENS = 4096
N_COL = 2


def block_scale(key, extent, split, smallest, high):
    loudness, own = 1.0, jax.random.fold_in(key, 6)
    for position, shards_of in split:
        steps = jnp.exp(jax.random.uniform(jax.random.fold_in(own, position), (shards_of,), jnp.float32, smallest / len(split), high / len(split)))
        loudness = loudness * jnp.repeat(steps, extent[position] // shards_of).reshape([-1 if axis == position else 1 for axis in range(len(extent))])
    return loudness


def centred(own_key, extent, scale, reach, split=(), held_as=jnp.bfloat16):
    entries = scale * jax.random.normal(own_key, extent, jnp.float32)
    if split:
        entries = entries * block_scale(own_key, extent, split, -0.22, 0.18)
    return jnp.clip(entries, -reach, reach).astype(held_as)


def setup_inputs(seed: int = 0) -> dict:
    splits = jax.random.split(jax.random.key(seed), 9)
    return {
        "errors": centred(splits[0], (TOKENS, D), (TOKENS // 16) ** -0.5, 0.375, ((0, 2), (1, 16))),
        "inputs": centred(splits[1], (TOKENS, D), 1.0, 6.0, ((0, 16), (1, 2))),
        "weight": centred(splits[2], (D, D), 0.5, 3.0, ((0, 16), (1, 2)), jnp.float32),
        "weight_moment_one": centred(splits[3], (D, D), 0.5, 3.0, ((0, 16), (1, 2))),
        "weight_moment_two": jnp.clip(jnp.exp(math.log(2.0) - 3.6927934 * jax.random.uniform(splits[4], (D, D), jnp.float32) ** block_scale(splits[4], (D, D), ((0, 16), (1, 2)), -0.2, 0.2)), 0.049804688, 2.0).astype(jnp.bfloat16),
        "feedback": centred(splits[5], (N_COL, D // N_COL, D), 0.5, 3.0, ((1, 16), (2, 2)), jnp.float32),
        "feedback_moment_one": centred(splits[6], (N_COL, D // N_COL, D), 0.5, 3.0, ((1, 16), (2, 2))),
        "feedback_moment_two": jnp.clip(jnp.exp(math.log(2.0) - 3.6927934 * jax.random.uniform(splits[7], (N_COL, D // N_COL, D), jnp.float32) ** block_scale(splits[7], (N_COL, D // N_COL, D), ((1, 16), (2, 2)), -0.2, 0.2)), 0.049804688, 2.0).astype(jnp.bfloat16),
    }


beta_one = 0.9
beta_two = 0.999
learn_rate = 0.02
decay_rate = 0.1
epsilon = 1e-08
bias_one = 1.0
bias_two = 0.63230458

def adam_update(master, moment_one, moment_two, gradient):
    first_new = beta_one * moment_one.astype(jnp.float32) + (1.0 - beta_one) * gradient
    second_new = beta_two * moment_two.astype(jnp.float32) + (1.0 - beta_two) * gradient * gradient
    update = first_new / bias_one / (jnp.sqrt(second_new / bias_two) + epsilon)
    master_new = master * (1.0 - learn_rate * decay_rate) - learn_rate * update
    return (master_new, first_new.astype(jnp.bfloat16), second_new.astype(jnp.bfloat16), master_new.astype(jnp.bfloat16))

def reference(errors, inputs, weight, weight_moment_one, weight_moment_two, feedback, feedback_moment_one, feedback_moment_two):
    gradient = jnp.dot(errors.astype(jnp.float32).T, inputs.astype(jnp.float32), precision=lax.Precision.HIGHEST)
    w_master, w_first, w_second, w_copy = adam_update(weight, weight_moment_one, weight_moment_two, gradient)
    flipped = gradient.T.reshape(feedback.shape)
    b_master, b_first, b_second, b_copy = adam_update(feedback, feedback_moment_one, feedback_moment_two, flipped)
    return (w_master, w_first, w_second, w_copy, b_master, b_first, b_second, b_copy)
```

```python
import functools

import jax
import jax.numpy as jnp
from jax import lax
from jax.experimental import pallas as pl
from jax.experimental.pallas import tpu as pltpu
from jax.sharding import PartitionSpec as P

beta_one = 0.9
beta_two = 0.999
learn_rate = 0.02
decay_rate = 0.1
epsilon = 1e-08
bias_one = 1.0
bias_two = 0.63230458

POWER = 11
HEAD = 11.5

QUAD = 4


def adam_update(master, moment_one, moment_two, gradient):
    first_new = beta_one * moment_one.astype(jnp.float32) + (1.0 - beta_one) * gradient
    second_new = beta_two * moment_two.astype(jnp.float32) + (1.0 - beta_two) * gradient * gradient
    update = first_new / bias_one / (jnp.sqrt(second_new / bias_two) + epsilon)
    master_new = master * (1.0 - learn_rate * decay_rate) - learn_rate * update
    return (
        master_new,
        first_new.astype(jnp.bfloat16),
        second_new.astype(jnp.bfloat16),
        master_new.astype(jnp.bfloat16),
    )


def encode(gradient, inverse):
    u = gradient * inverse
    u2 = u * u
    u4 = u2 * u2
    return (u4 * u4 * u2 * u).astype(jnp.bfloat16)


def decode(code, scale):
    y = code.astype(jnp.float32)
    size = jnp.exp(jnp.log(jnp.abs(y)) * (1.0 / POWER)) * scale
    return jnp.where(y > 0.0, size, jnp.where(y < 0.0, -size, 0.0))


def my_place():
    row = lax.axis_index("row")
    return row // QUAD, row % QUAD, lax.axis_index("col")


def scalar_spec():
    return pl.BlockSpec(memory_space=pltpu.SMEM)


def any_specs(n):
    return [pl.BlockSpec(memory_space=pl.ANY)] * n


def product_kernel(line, n_col, tokens, outputs, error_at, n_errors, inverse_ref, *refs):
    share = line // n_col
    candidates, refs = refs[: 2 * line - 1], refs[2 * line - 1 :]
    errors, refs = refs[:n_errors], refs[n_errors:]
    to_line, to_quad, refs = refs[:line], refs[line : line + QUAD], refs[line + QUAD :]
    held, turned, whole, code, in_sem, error_sem, out_sem = refs
    layer, quarter, column = my_place()
    depth = QUAD * tokens
    width = held.shape[1]
    rows = width // line

    for n in range(line):
        source = (column ^ (n // share)) * share + n % share
        for i, candidate in enumerate(candidates):
            copy = pltpu.make_async_copy(candidate, held.at[pl.ds(n * depth, depth)], in_sem.at[n])
            pl.when(source - layer == i - (line - 1))(copy.start)
    for q in range(QUAD):
        for n in range(line):
            for d in range(QUAD):
                ref, start = error_at(n // share, q, n % share, quarter ^ d, column)
                pltpu.make_async_copy(
                    errors[ref].at[pl.ds(pl.multiple_of(start, tokens), tokens)],
                    whole.at[pl.ds(n * depth + d * tokens, tokens), pl.ds(q * outputs, outputs)],
                    error_sem.at[q],
                ).start()
    for n in range(line):
        part = held.at[pl.ds(n * depth, depth)]
        pltpu.make_async_copy(part, part, in_sem.at[n]).wait()

    step = 256 if width % 256 == 0 else width
    for w in range(width // step):

        @pl.loop(0, line * depth // 256)
        def _(i):
            at = pl.multiple_of(i * 256, 256)
            turned[:, pl.ds(at, 256)] = held[pl.ds(at, 256), pl.ds(w * step, step)].T

        for q in range(QUAD):
            part = whole.at[:, pl.ds(q * outputs, outputs)]
            if w == 0:
                pltpu.make_async_copy(part, part, error_sem.at[q]).wait()
            gradient = jnp.dot(turned[...], part[...], preferred_element_type=jnp.float32)
            code[pl.ds(w * step, step), pl.ds(q * outputs, outputs)] = encode(gradient, inverse_ref[0])

    copies = []
    for j in range(line):
        to = ((layer % share) * n_col + column) ^ j
        copies.append((code.at[pl.ds(pl.multiple_of(to * rows, 16), rows)], to_line[j]))
    for d in range(QUAD):
        copies.append((code.at[:, pl.ds(d * outputs, outputs)], to_quad[d]))
    copies = [pltpu.make_async_copy(a, b, out_sem.at[i]) for i, (a, b) in enumerate(copies)]
    for copy in copies:
        copy.start()
    for copy in copies:
        copy.wait()


def product(line, n_col, tokens, outputs, error_at, inverse, candidates, errors):
    width = candidates[0].shape[1]
    whole = (line * QUAD * tokens, QUAD * outputs)
    return pl.pallas_call(
        functools.partial(product_kernel, line, n_col, tokens, outputs, error_at, len(errors)),
        out_shape=[jax.ShapeDtypeStruct((width // line, QUAD * outputs), jnp.bfloat16)] * line
        + [jax.ShapeDtypeStruct((width, outputs), jnp.bfloat16)] * QUAD,
        in_specs=[scalar_spec()] + any_specs(len(candidates) + len(errors)),
        out_specs=any_specs(line + QUAD),
        scratch_shapes=[
            pltpu.VMEM((line * QUAD * tokens, width), jnp.bfloat16),
            pltpu.VMEM((256 if width % 256 == 0 else width, line * QUAD * tokens), jnp.bfloat16),
            pltpu.VMEM(whole, jnp.bfloat16),
            pltpu.VMEM((width, QUAD * outputs), jnp.bfloat16),
            pltpu.SemaphoreType.DMA((line,)),
            pltpu.SemaphoreType.DMA((QUAD,)),
            pltpu.SemaphoreType.DMA((line + QUAD,)),
        ],
        compiler_params=pltpu.CompilerParams(vmem_limit_bytes=56 * 2**20),
        cost_estimate=pl.CostEstimate(
            flops=2 * width * whole[0] * whole[1], bytes_accessed=2 * whole[0] * (whole[1] + width), transcendentals=0
        ),
        name="product",
    )(inverse, *candidates, *errors)


def weight_kernel(line, lows, scale_ref, *refs):
    n = len(lows)
    pieces, refs = refs[: n * QUAD], refs[n * QUAD :]
    master, one, two = refs[:3]
    outs, (held, sem) = refs[3:7], refs[7:]
    _, quarter, _ = my_place()

    @pl.when(pl.program_id(0) == 0)
    def _():
        copies = []
        for p, low in enumerate(lows):
            for d in range(QUAD):
                rows = pieces[p * QUAD + d].shape[0] // line
                for h in range(line):
                    copies.append(
                        pltpu.make_async_copy(
                            pieces[p * QUAD + d].at[pl.ds(h * rows, rows)],
                            held.at[h, quarter ^ d, pl.ds(low, rows)],
                            sem.at[len(copies)],
                        )
                    )
        for copy in copies:
            copy.start()
        for copy in copies:
            copy.wait()

    code = held[pl.program_id(0)]
    gradient = decode(code.reshape(code.shape[0] * code.shape[1], code.shape[2]), scale_ref[0]).T
    for out, value in zip(outs, adam_update(master[...], one[...], two[...], gradient)):
        out[...] = value


def weight_update(line, lows, scale, pieces, master, one, two):
    outputs, columns = master.shape
    tile = pl.BlockSpec((outputs, columns // line), lambda h: (0, h))
    return pl.pallas_call(
        functools.partial(weight_kernel, line, lows),
        grid=(line,),
        out_shape=[
            jax.ShapeDtypeStruct(master.shape, t) for t in (jnp.float32, jnp.bfloat16, jnp.bfloat16, jnp.bfloat16)
        ],
        in_specs=[scalar_spec()] + any_specs(len(pieces)) + [tile] * 3,
        out_specs=[tile] * 4,
        scratch_shapes=[
            pltpu.VMEM((line, QUAD, columns // line // QUAD, outputs), jnp.bfloat16),
            pltpu.SemaphoreType.DMA((len(lows) * QUAD * line,)),
        ],
        compiler_params=pltpu.CompilerParams(vmem_limit_bytes=56 * 2**20),
        cost_estimate=pl.CostEstimate(flops=0, bytes_accessed=20 * master.size, transcendentals=3 * master.size),
        name="weight_update",
    )(scale, *pieces, master, one, two)


def feedback_kernel(line, n_col, n_held, scale_ref, *refs):
    share = line // n_col
    pieces, refs = refs[:line], refs[line:]
    (master, one, two), refs = refs[:3], refs[3 + n_held :]
    outs, (held, sem) = refs[:4], refs[4:]
    layer, quarter, _ = my_place()
    outputs = held.shape[-1]

    @pl.when((pl.program_id(0) == 0) & (pl.program_id(1) == 0))
    def _():
        copies = []
        for j in range(line):
            source = layer ^ j
            for d in range(QUAD):
                copies.append(
                    pltpu.make_async_copy(
                        pieces[j].at[:, pl.ds(d * outputs, outputs)],
                        held.at[source % n_col, source // n_col, quarter ^ d],
                        sem.at[len(copies)],
                    )
                )
        for copy in copies:
            copy.start()
        for copy in copies:
            copy.wait()

    rows = master.shape[1]
    at = pl.ds(pl.multiple_of(pl.program_id(1) * rows, 16), rows)
    for s in range(share):
        for q in range(QUAD):
            lanes = pl.ds((s * QUAD + q) * outputs, outputs)
            gradient = decode(held[pl.program_id(0), s, q, at, :], scale_ref[0])
            values = adam_update(master[0, :, lanes], one[0, :, lanes], two[0, :, lanes], gradient)
            for out, value in zip(outs, values):
                out[0, :, lanes] = value


def feedback_update(line, n_col, low, scale, pieces, master, one, two, held):
    groups, _, width = master.shape
    span = pieces[0].shape[0]
    rows = 32 if span % 32 == 0 and low % 32 == 0 else 16
    tile = pl.BlockSpec((1, rows, width), lambda g, t: (g, low // rows + t, 0))
    return pl.pallas_call(
        functools.partial(feedback_kernel, line, n_col, len(held)),
        grid=(groups, span // rows),
        out_shape=[
            jax.ShapeDtypeStruct(master.shape, t) for t in (jnp.float32, jnp.bfloat16, jnp.bfloat16, jnp.bfloat16)
        ],
        in_specs=[scalar_spec()] + any_specs(line) + [tile] * 3 + any_specs(len(held)),
        out_specs=[tile] * 4,
        scratch_shapes=[
            pltpu.VMEM((n_col, line // n_col, QUAD, span, pieces[0].shape[1] // QUAD), jnp.bfloat16),
            pltpu.SemaphoreType.DMA((line * QUAD,)),
        ],
        input_output_aliases={1 + line + 3 + i: i for i in range(len(held))},
        compiler_params=pltpu.CompilerParams(vmem_limit_bytes=56 * 2**20),
        cost_estimate=pl.CostEstimate(
            flops=0, bytes_accessed=20 * groups * span * width, transcendentals=3 * groups * span * width
        ),
        name="feedback_update",
    )(scale, *pieces, master, one, two, *held)


def make(n_row, n_col):
    line = n_row // QUAD
    share = line // n_col

    def permute(x, move):
        pairs = []
        for r in range(n_row):
            for c in range(n_col):
                to = move(r // QUAD, r % QUAD, c)
                if to is not None:
                    pairs.append((r * n_col + c, (to[0] * QUAD + to[1]) * n_col + to[2]))
        return lax.ppermute(x, ("row", "col"), pairs)

    def along_quad(x, d):
        return permute(x, lambda h, q, c: (h, q ^ d, c))

    def along_col(x, d):
        return permute(x, lambda h, q, c: (h, q, c ^ d))

    def up(x, k):
        return permute(x, lambda h, q, c: (h + 1, q, c) if k <= h < line - 1 else None)

    def down(x, k):
        return permute(x, lambda h, q, c: (h - 1, q, c) if 0 < h < line - k else None)

    def gather_errors(errors, tokens):
        if n_col != 2:
            mine = lax.all_gather(errors, "col", axis=0, tiled=True)
            pieces = [mine] + [along_quad(mine, d) for d in range(1, QUAD)]

            def error_at(dc, dq, s, q, column):
                return dq, (((column ^ dc) * share + s) * QUAD + q) * tokens

            return pieces, error_at
        half = errors.shape[0] // 2
        by_col, by_x = along_col(errors, 1), along_quad(errors, 2)
        by_both = along_quad(by_col[:half], 2), along_col(by_x[half:], 1)
        near = [errors, by_col, by_x, *by_both]
        pieces = near + [along_quad(piece, 1) for piece in near]

        def error_at(dc, dq, s, q, column):
            core, x = dq % 2, dq // 2
            if dc and x and share > 1:
                late = s // (share // 2)
                return core * 5 + 3 + late, ((s - late * (share // 2)) * QUAD + q) * tokens
            return core * 5 + x * 2 + dc, (s * QUAD + q) * tokens

        return pieces, error_at

    def shards(
        errors,
        inputs,
        weight,
        weight_moment_one,
        weight_moment_two,
        feedback,
        feedback_moment_one,
        feedback_moment_two,
    ):
        layer, quarter, column = my_place()
        tokens = inputs.shape[0]
        block = inputs.shape[1] // n_row
        outputs = errors.shape[1]
        split = block * 3 // 4 // 16 * 16
        parts = ((0, split), (split, block))

        largest = jnp.stack([jnp.max(jnp.abs(errors)), jnp.max(jnp.abs(inputs))]).astype(jnp.float32)
        largest = lax.all_gather(jnp.broadcast_to(largest[:, None], (2, 128)), ("row", "col"), axis=0)
        largest = jnp.max(largest, axis=(0, 2))
        bound = largest[0] * largest[1] * (n_row * tokens)
        bound = jnp.where(bound > 0.0, bound, 1.0)
        inverse, scale = (2.0**HEAD / bound)[None], (bound * 2.0**-HEAD)[None]

        columns = inputs.reshape(tokens, line, QUAD, block)

        def of(q):
            taken = lax.dynamic_index_in_dim(columns, q, 2, keepdims=False)
            return jnp.concatenate([taken[:, :, a:b].reshape(tokens, -1) for a, b in parts], axis=1)

        own = [of(quarter)] + [along_quad(of(quarter ^ d), d) for d in range(1, QUAD)]
        gathered = []
        for a, b in parts:
            start = jnp.concatenate([piece[:, line * a : line * b] for piece in own], axis=0)
            ups, downs = [start], [start]
            for k in range(line - 1):
                ups.append(up(ups[-1], k))
                downs.append(down(downs[-1], k))
            gathered.append(ups[:0:-1] + downs)
        pieces, error_at = gather_errors(errors, tokens)

        for_weight, new_feedback = [], []
        for (a, b), candidates in zip(parts, gathered):
            codes = product(line, n_col, tokens, outputs, error_at, inverse, candidates, pieces)
            for_feedback = [
                permute(code, lambda h, q, c: (((h % share) * n_col + c) ^ j, q, h // share))
                for j, code in enumerate(codes[:line])
            ]
            for_weight += [along_quad(code, d) if d else code for d, code in enumerate(codes[line:])]
            new_feedback = feedback_update(
                line,
                n_col,
                a,
                scale,
                for_feedback,
                feedback,
                feedback_moment_one,
                feedback_moment_two,
                new_feedback,
            )
        new_weight = weight_update(
            line, tuple(a for a, _ in parts), scale, for_weight, weight, weight_moment_one, weight_moment_two
        )
        return (*new_weight, *new_feedback)

    return shards


def solution(mesh):
    forward, backward = P("row", "col"), P(None, "row", "col")
    return jax.shard_map(
        make(mesh.shape["row"], mesh.shape["col"]),
        mesh=mesh,
        in_specs=(P("col", "row"), forward, forward, forward, forward, backward, backward, backward),
        out_specs=(forward,) * 4 + (backward,) * 4,
        check_vma=False,
    )
```

```python
import functools
import math

import jax
import jax.numpy as jnp
from jax import lax
from jax.experimental import pallas as pl
from jax.experimental.pallas import tpu as pltpu
from jax.sharding import PartitionSpec as P

beta_one = 0.9
beta_two = 0.999
learn_rate = 0.02
decay_rate = 0.1
epsilon = 1e-08
bias_one = 1.0
bias_two = 0.63230458

POWER = 13
HEAD = 9.7

BRIEF = pl.CostEstimate(flops=0, bytes_accessed=0, transcendentals=0)

QUAD = 4


def adam_update(master, moment_one, moment_two, gradient):
    first_new = beta_one * moment_one.astype(jnp.float32) + (1.0 - beta_one) * gradient
    second_new = beta_two * moment_two.astype(jnp.float32) + (1.0 - beta_two) * gradient * gradient
    corrected = second_new * (1.0 / bias_two)
    divisor = corrected * lax.rsqrt(corrected) + epsilon
    inverse = pl.reciprocal(divisor, approx=True)
    inverse = inverse * (2.0 - divisor * inverse)
    master_new = master * (1.0 - learn_rate * decay_rate) - (learn_rate / bias_one) * first_new * inverse
    return (
        master_new,
        first_new.astype(jnp.bfloat16),
        second_new.astype(jnp.bfloat16),
        master_new.astype(jnp.bfloat16),
    )


def encode(gradient, inverse):
    u = gradient * inverse
    u2 = u * u
    u4 = u2 * u2
    return (u4 * u4 * u4 * u).astype(jnp.bfloat16)


def decode(code, scale):
    y = code.astype(jnp.float32)
    size = jnp.exp2(jnp.log(jnp.abs(y)) * (1.0 / (POWER * math.log(2.0)))) * scale
    return jnp.where(y < 0.0, -size, size)


def slot(layer, column, share):
    return column * share + (layer + column) % share


def unslot(index, share):
    return index // share, (index + index // share * (share - 1)) % share


def my_place():
    row = lax.axis_index("row")
    return row // QUAD, row % QUAD, lax.axis_index("col")


def scalar_spec():
    return pl.BlockSpec(memory_space=pltpu.SMEM)


def any_specs(n):
    return [pl.BlockSpec(memory_space=pl.ANY)] * n


def after(value, *others):
    return lax.optimization_barrier((value, *others))[0]


def pack_kernel(line, x_ref, *outs):
    _, quarter, _ = my_place()
    block = x_ref.shape[1] // (line * QUAD)
    for d, out in enumerate(outs):
        for h in range(line):
            start = pl.multiple_of((h * QUAD + (quarter ^ d)) * block, block)
            out[:, pl.ds(h * block, block)] = x_ref[:, pl.ds(start, block)]


def pack(line, x):
    return pl.pallas_call(
        functools.partial(pack_kernel, line),
        out_shape=[jax.ShapeDtypeStruct((x.shape[0], x.shape[1] // QUAD), x.dtype)] * QUAD,
        in_specs=[pl.BlockSpec(memory_space=pltpu.VMEM)],
        out_specs=[pl.BlockSpec(memory_space=pltpu.VMEM)] * QUAD,
        compiler_params=pltpu.CompilerParams(vmem_limit_bytes=32 * 2**20),
        cost_estimate=BRIEF,
        name="pack",
    )(x)


def product_kernel(line, n_col, tokens, outputs, depths, inverse_ref, *refs):
    share = line // n_col
    reach = 2 * line - 1
    candidates, refs = refs[: len(depths) * reach], refs[len(depths) * reach :]
    errors, refs = refs[0], refs[1:]
    to_line, to_quad, refs = refs[:line], refs[line : line + QUAD], refs[line + QUAD :]
    held, turned, whole, code, in_sem, error_sem, out_sem = refs
    layer, quarter, column = my_place()
    depth = QUAD * tokens
    width = held.shape[1]
    rows = width // line

    for n in range(line):
        source = (column ^ (n // share)) * share + n % share
        start = n * depth
        for g, slab in enumerate(depths):
            for i, candidate in enumerate(candidates[g * reach : (g + 1) * reach]):
                copy = pltpu.make_async_copy(candidate, held.at[pl.ds(start, slab)], in_sem.at[n])
                pl.when(source - layer == i - (line - 1))(copy.start)
            start += slab
    for q in range(QUAD):
        for n in range(line):
            for d in range(QUAD):
                start = (column ^ (n // share)) * QUAD + (quarter ^ q)
                start = ((start * share + n % share) * QUAD + (quarter ^ d)) * tokens
                pltpu.make_async_copy(
                    errors.at[pl.ds(pl.multiple_of(start, tokens), tokens)],
                    whole.at[pl.ds(n * depth + d * tokens, tokens), pl.ds(q * outputs, outputs)],
                    error_sem.at[q],
                ).start()
    for n in range(line):
        part = held.at[pl.ds(n * depth, depth)]
        pltpu.make_async_copy(part, part, in_sem.at[n]).wait()

        @pl.loop(n * depth // 256, (n + 1) * depth // 256)
        def _(i):
            at = pl.multiple_of(i * 256, 256)
            turned[:, pl.ds(at, 256)] = held[pl.ds(at, 256), :].T

    copies = []
    for q in range(QUAD):
        lanes = pl.ds(q * outputs, outputs)
        part = whole.at[:, lanes]
        pltpu.make_async_copy(part, part, error_sem.at[q]).wait()
        gradient = jnp.dot(turned[...], part[...], preferred_element_type=jnp.float32)
        code[:, lanes] = encode(gradient, inverse_ref[0])
        ready = [(code.at[:, lanes], to_quad[q])]
        for j in range(line):
            to = slot(layer, column, share) ^ j
            at = pl.ds(pl.multiple_of(to * rows, 16), rows)
            ready.append((code.at[at, lanes], to_line[j].at[:, lanes]))
        for source, target in ready:
            copies.append(pltpu.make_async_copy(source, target, out_sem.at[len(copies)]))
            copies[-1].start()
    for copy in copies:
        copy.wait()


def product(line, n_col, tokens, outputs, inverse, groups, errors):
    width = groups[0][0].shape[1]
    whole = (line * QUAD * tokens, QUAD * outputs)
    depths = [group[0].shape[0] for group in groups]
    candidates = [candidate for group in groups for candidate in group]
    return pl.pallas_call(
        functools.partial(product_kernel, line, n_col, tokens, outputs, depths),
        out_shape=[jax.ShapeDtypeStruct((width // line, QUAD * outputs), jnp.bfloat16)] * line
        + [jax.ShapeDtypeStruct((width, outputs), jnp.bfloat16)] * QUAD,
        in_specs=[scalar_spec()] + any_specs(len(candidates) + 1),
        out_specs=any_specs(line + QUAD),
        scratch_shapes=[
            pltpu.VMEM((line * QUAD * tokens, width), jnp.bfloat16),
            pltpu.VMEM((width, line * QUAD * tokens), jnp.bfloat16),
            pltpu.VMEM(whole, jnp.bfloat16),
            pltpu.VMEM((width, QUAD * outputs), jnp.bfloat16),
            pltpu.SemaphoreType.DMA((line,)),
            pltpu.SemaphoreType.DMA((QUAD,)),
            pltpu.SemaphoreType.DMA(((line + 1) * QUAD,)),
        ],
        compiler_params=pltpu.CompilerParams(vmem_limit_bytes=56 * 2**20),
        cost_estimate=BRIEF,
        name="product",
    )(inverse, *candidates, errors)


def weight_kernel(line, scale_ref, *refs):
    pieces, refs = refs[:QUAD], refs[QUAD:]
    master, one, two = refs[:3]
    outs, (held, sem) = refs[3:7], refs[7:]
    _, quarter, _ = my_place()

    @pl.when(pl.program_id(0) == 0)
    def _():
        copies = []
        for d, piece in enumerate(pieces):
            rows = piece.shape[0] // line
            for h in range(line):
                source, target = piece.at[pl.ds(h * rows, rows)], held.at[h, quarter ^ d]
                copies.append(pltpu.make_async_copy(source, target, sem.at[len(copies)]))
        for copy in copies:
            copy.start()
        for copy in copies:
            copy.wait()

    code = held[pl.program_id(0)]
    gradient = decode(code.reshape(code.shape[0] * code.shape[1], code.shape[2]), scale_ref[0]).T
    for out, value in zip(outs, adam_update(master[...], one[...], two[...], gradient)):
        out[...] = value


def weight_update(line, scale, pieces, master, one, two):
    outputs, columns = master.shape
    tile = pl.BlockSpec((outputs, columns // line), lambda h: (0, h))
    return pl.pallas_call(
        functools.partial(weight_kernel, line),
        grid=(line,),
        out_shape=[
            jax.ShapeDtypeStruct(master.shape, t) for t in (jnp.float32, jnp.bfloat16, jnp.bfloat16, jnp.bfloat16)
        ],
        in_specs=[scalar_spec()] + any_specs(len(pieces)) + [tile] * 3,
        out_specs=[tile] * 4,
        scratch_shapes=[
            pltpu.VMEM((line, QUAD, columns // line // QUAD, outputs), jnp.bfloat16),
            pltpu.SemaphoreType.DMA((QUAD * line,)),
        ],
        compiler_params=pltpu.CompilerParams(vmem_limit_bytes=56 * 2**20),
        cost_estimate=BRIEF,
        name="weight_update",
    )(scale, *pieces, master, one, two)


def feedback_kernel(line, odd, n_held, _, scale_ref, *refs):
    pieces, refs = refs[: line // 2], refs[line // 2 :]
    (master, one, two), refs = refs[:3], refs[3 + n_held :]
    outs, (held, sem) = refs[:4], refs[4:]
    layer, quarter, _ = my_place()
    outputs = held.shape[-1]

    @pl.when((pl.program_id(0) == 0) & (pl.program_id(1) == 0))
    def _():
        copies = []
        for i, piece in enumerate(pieces):
            half = (layer ^ (2 * i + odd)) // 2
            for d in range(QUAD):
                source, target = piece.at[:, pl.ds(d * outputs, outputs)], held.at[half, quarter ^ d]
                copies.append(pltpu.make_async_copy(source, target, sem.at[len(copies)]))
        for copy in copies:
            copy.start()
        for copy in copies:
            copy.wait()

    rows = master.shape[1]
    at = pl.ds(pl.multiple_of(pl.program_id(1) * rows, 16), rows)
    for q in range(QUAD):
        lanes = pl.ds(q * outputs, outputs)
        gradient = decode(held[pl.program_id(0), q, at, :], scale_ref[0])
        values = adam_update(master[0, :, lanes], one[0, :, lanes], two[0, :, lanes], gradient)
        for out, value in zip(outs, values):
            out[0, :, lanes] = value


def feedback_update(line, share, odd, scale, pieces, master, one, two, held):
    block, width = master.shape[1], master.shape[2] // share
    rows = 64 if block % 64 == 0 else block

    def place(i, t, first):
        group, s = unslot(2 * i + first[0], share)
        return group, t, s

    tile = pl.BlockSpec((1, rows, width), place)
    first = ((my_place()[0] ^ odd) % 2)[None].astype(jnp.int32)
    return pl.pallas_call(
        functools.partial(feedback_kernel, line, odd, len(held)),
        grid_spec=pltpu.PrefetchScalarGridSpec(
            num_scalar_prefetch=1,
            grid=(line // 2, block // rows),
            in_specs=[scalar_spec()] + any_specs(line // 2) + [tile] * 3 + any_specs(len(held)),
            out_specs=[tile] * 4,
            scratch_shapes=[
                pltpu.VMEM((line // 2, QUAD, block, width // QUAD), jnp.bfloat16),
                pltpu.SemaphoreType.DMA((line // 2 * QUAD,)),
            ],
        ),
        out_shape=[
            jax.ShapeDtypeStruct(master.shape, t) for t in (jnp.float32, jnp.bfloat16, jnp.bfloat16, jnp.bfloat16)
        ],
        input_output_aliases={2 + line // 2 + 3 + i: i for i in range(len(held))},
        compiler_params=pltpu.CompilerParams(vmem_limit_bytes=56 * 2**20),
        cost_estimate=BRIEF,
        name="feedback_update",
    )(first, scale, *pieces, master, one, two, *held)


def make(n_row, n_col):
    line = n_row // QUAD
    share = line // n_col

    def permute(x, move):
        pairs = []
        for r in range(n_row):
            for c in range(n_col):
                to = move(r // QUAD, r % QUAD, c)
                if to is not None:
                    pairs.append((r * n_col + c, (to[0] * QUAD + to[1]) * n_col + to[2]))
        return lax.ppermute(x, ("row", "col"), pairs)

    def flipped_pairs(bit):
        return [(i, i ^ bit) for i in range(n_row * n_col)]

    def along_quad(x, d):
        return permute(x, lambda h, q, c: (h, q ^ d, c))

    def along_col(x, d):
        return permute(x, lambda h, q, c: (h, q, c ^ d))

    def up(x, k):
        return permute(x, lambda h, q, c: (h + 1, q, c) if k <= h < line - 1 else None)

    def down(x, k):
        return permute(x, lambda h, q, c: (h - 1, q, c) if 0 < h < line - k else None)

    layers = [
        [(h * QUAD + q) * n_col + c for c in range(n_col) for q in range(QUAD)] for h in range(line)
    ]

    def shards(
        errors,
        inputs,
        weight,
        weight_moment_one,
        weight_moment_two,
        feedback,
        feedback_moment_one,
        feedback_moment_two,
    ):
        layer, quarter, column = my_place()
        tokens = inputs.shape[0]
        block = inputs.shape[1] // n_row
        outputs = errors.shape[1]

        squares = [jnp.max(jnp.sum(jnp.square(x.astype(jnp.float32) * 2.0**40), axis=0)) for x in (errors, inputs)]
        squares = jnp.stack(squares)
        squares_of_line = ()
        for bit in reversed(range((n_row * n_col).bit_length() - 1)):
            if (1 << bit) < n_col * QUAD and not isinstance(squares_of_line, jax.Array):
                squares_of_line = squares
            others = lax.ppermute(squares, ("row", "col"), flipped_pairs(1 << bit))
            added = jnp.array([(1 << bit) < n_col, (1 << bit) >= n_col])
            squares = jnp.where(added, squares + others, jnp.maximum(squares, others))
        lengths = jnp.sqrt(squares) * 2.0**-40
        bound = lengths[0] * lengths[1] * 1.01
        bound = jnp.where(bound > 0.0, bound, 1.0)
        inverse, scale = (2.0**HEAD / bound)[None], (bound * 2.0**-HEAD)[None]

        if block % 128 == 0:
            own = pack(line, inputs)
        else:
            columns = inputs.reshape(tokens, line, QUAD, block)
            own = [
                lax.dynamic_index_in_dim(columns, quarter ^ d, 2, keepdims=False).reshape(tokens, line * block)
                for d in range(QUAD)
            ]
        own = [own[0]] + [along_quad(own[d], d) for d in range(1, QUAD)]

        def along_line(start):
            ups, downs = [start], [start]
            for k in range(line - 1):
                ups.append(up(ups[-1], k))
                downs.append(down(downs[-1], k))
            return ups[:0:-1] + downs

        near = along_line(jnp.concatenate([own[0], after(own[1], squares_of_line)], axis=0))
        start = jnp.concatenate([after(own[2], near[line - 2], near[line]), own[3]], axis=0)
        far = along_line(start)
        whole_errors = lax.all_gather(
            after(errors, start), ("row", "col"), axis=0, tiled=True, axis_index_groups=layers
        )
        codes = product(line, n_col, tokens, outputs, inverse, (near, far), whole_errors)
        for_feedback = {}
        for j in (*range(0, line, 2), *range(1, line, 2)):
            code = codes[j]
            if j % 2:
                code = after(code, for_feedback[j - 1])
            for_feedback[j] = permute(code, lambda h, q, c: (slot(h, c, share) ^ j, q, h // share))
        for_weight = [along_quad(code, d) if d else code for d, code in enumerate(codes[line:])]

        def update_feedback(odd, held, *others):
            return feedback_update(
                line,
                share,
                odd,
                after(scale, *others),
                [for_feedback[j] for j in range(odd, line, 2)],
                feedback,
                feedback_moment_one,
                feedback_moment_two,
                held,
            )

        new_feedback = update_feedback(0, [])
        new_weight = weight_update(
            line, after(scale, new_feedback[1]), for_weight, weight, weight_moment_one, weight_moment_two
        )
        new_feedback = update_feedback(1, new_feedback, new_weight[1])
        return (*new_weight, *new_feedback)

    return shards


def solution(mesh):
    forward, backward = P("row", "col"), P(None, "row", "col")
    return jax.shard_map(
        make(mesh.shape["row"], mesh.shape["col"]),
        mesh=mesh,
        in_specs=(P("col", "row"), forward, forward, forward, forward, backward, backward, backward),
        out_specs=(forward,) * 4 + (backward,) * 4,
        check_vma=False,
    )
```

```python
import functools
import math

import jax
import jax.numpy as jnp
from jax import lax
from jax.experimental import pallas as pl
from jax.experimental.pallas import tpu as pltpu
from jax.sharding import PartitionSpec as P

beta_one = 0.9
beta_two = 0.999
learn_rate = 0.02
decay_rate = 0.1
epsilon = 1e-08
bias_one = 1.0
bias_two = 0.63230458

POWER = 13
HEAD = 9.7

BRIEF = pl.CostEstimate(flops=0, bytes_accessed=0, transcendentals=0)

QUAD = 4


def adam_update(master, moment_one, moment_two, gradient):
    first_new = beta_one * moment_one.astype(jnp.float32) + (1.0 - beta_one) * gradient
    second_new = beta_two * moment_two.astype(jnp.float32) + (1.0 - beta_two) * gradient * gradient
    corrected = second_new * (1.0 / bias_two)
    divisor = corrected * lax.rsqrt(corrected) + epsilon
    inverse = pl.reciprocal(divisor, approx=True)
    inverse = inverse * (2.0 - divisor * inverse)
    master_new = master * (1.0 - learn_rate * decay_rate) - (learn_rate / bias_one) * first_new * inverse
    return (
        master_new,
        first_new.astype(jnp.bfloat16),
        second_new.astype(jnp.bfloat16),
        master_new.astype(jnp.bfloat16),
    )


def encode(gradient, inverse):
    u = gradient * inverse
    u2 = u * u
    u4 = u2 * u2
    return (u4 * u4 * u4 * u).astype(jnp.bfloat16)


def decode(code, scale):
    y = code.astype(jnp.float32)
    size = jnp.exp2(jnp.log(jnp.abs(y)) * (1.0 / (POWER * math.log(2.0)))) * scale
    return jnp.where(y < 0.0, -size, size)


def slot(layer, column, share):
    return column * share + (layer + column) % share


def unslot(index, share):
    return index // share, (index + index // share * (share - 1)) % share


def my_place():
    row = lax.axis_index("row")
    return row // QUAD, row % QUAD, lax.axis_index("col")


def scalar_spec():
    return pl.BlockSpec(memory_space=pltpu.SMEM)


def any_specs(n):
    return [pl.BlockSpec(memory_space=pl.ANY)] * n


def after(value, *others):
    return lax.optimization_barrier((value, *others))[0]


def pack_kernel(line, x_ref, *outs):
    _, quarter, _ = my_place()
    block = x_ref.shape[1] // (line * QUAD)
    for d, out in enumerate(outs):
        for h in range(line):
            start = pl.multiple_of((h * QUAD + (quarter ^ d)) * block, block)
            out[:, pl.ds(h * block, block)] = x_ref[:, pl.ds(start, block)]


def pack(line, x):
    return pl.pallas_call(
        functools.partial(pack_kernel, line),
        out_shape=[jax.ShapeDtypeStruct((x.shape[0], x.shape[1] // QUAD), x.dtype)] * QUAD,
        in_specs=[pl.BlockSpec(memory_space=pltpu.VMEM)],
        out_specs=[pl.BlockSpec(memory_space=pltpu.VMEM)] * QUAD,
        compiler_params=pltpu.CompilerParams(vmem_limit_bytes=32 * 2**20),
        cost_estimate=BRIEF,
        name="pack",
    )(x)


def longest_kernel(errors_ref, inputs_ref, out_ref):
    for half, ref in enumerate((errors_ref, inputs_ref)):
        total = jnp.zeros((1, ref.shape[1]), jnp.float32)
        step = min(256, ref.shape[0])
        for start in range(0, ref.shape[0], step):
            x = ref[pl.ds(start, step), :].astype(jnp.float32) * 2.0**40
            total = total + jnp.sum(x * x, axis=0, keepdims=True)
        out_ref[pl.ds(half * 4, 4), :] = jnp.broadcast_to(jnp.max(total, axis=1, keepdims=True), (4, 128))


def longest(errors, inputs):
    return pl.pallas_call(
        longest_kernel,
        out_shape=jax.ShapeDtypeStruct((8, 128), jnp.float32),
        in_specs=[pl.BlockSpec(memory_space=pltpu.VMEM)] * 2,
        out_specs=pl.BlockSpec(memory_space=pltpu.VMEM),
        compiler_params=pltpu.CompilerParams(vmem_limit_bytes=32 * 2**20),
        cost_estimate=BRIEF,
        name="longest",
    )(errors, inputs)


def product_kernel(line, n_col, tokens, outputs, slab, picks, n_old, inverse_ref, *refs):
    share = line // n_col
    candidates, refs = refs[: 2 * line - 1], refs[2 * line - 1 :]
    errors, refs = refs[0], refs[1:]
    layer, quarter, column = my_place()
    depth = len(slab) * tokens
    block = candidates[0].shape[1] // line
    if picks:
        so_far, refs = refs[0], refs[1 + n_old :]
        to_line, to_quad, refs = refs[: len(picks)], refs[len(picks) : len(picks) + QUAD], refs[len(picks) + QUAD :]
        held, turned, whole, total, code, in_sem, error_sem, total_sem, out_sem = refs
    else:
        result, held, turned, whole, total, in_sem, error_sem, out_sem = refs
    apart = picks and len(picks) < line
    layers = [slot(layer, column, share) ^ j for j in picks or ()]
    spans = [pl.ds(pl.multiple_of(to * block, block), block) for to in layers]

    for n in range(line):
        source = (column ^ (n // share)) * share + n % share
        for i, candidate in enumerate(candidates):

            @pl.when(source - layer == i - (line - 1))
            def _():
                rows = pl.ds(n * depth, depth)
                if apart:
                    for m, span in enumerate(spans):
                        part = held.at[rows, pl.ds(m * block, block)]
                        pltpu.make_async_copy(candidate.at[:, span], part, in_sem.at[n]).start()
                else:
                    pltpu.make_async_copy(candidate, held.at[rows], in_sem.at[n]).start()

    for q in range(QUAD):
        for n in range(line):
            for m, d in enumerate(slab):
                start = (column ^ (n // share)) * QUAD + (quarter ^ q)
                start = ((start * share + n % share) * QUAD + (quarter ^ d)) * tokens
                pltpu.make_async_copy(
                    errors.at[pl.ds(pl.multiple_of(start, tokens), tokens)],
                    whole.at[pl.ds(n * depth + m * tokens, tokens), pl.ds(q * outputs, outputs)],
                    error_sem.at[q],
                ).start()
    if apart:
        for m, span in enumerate(spans):
            pltpu.make_async_copy(so_far.at[span], total.at[pl.ds(m * block, block)], total_sem).start()
    elif picks:
        pltpu.make_async_copy(so_far, total, total_sem).start()

    for n in range(line):
        part = held.at[pl.ds(n * depth, depth)]
        pltpu.make_async_copy(part, part, in_sem.at[n]).wait()

        @pl.loop(n * depth // 256, (n + 1) * depth // 256)
        def _(i):
            at = pl.multiple_of(i * 256, 256)
            turned[:, pl.ds(at, 256)] = held[pl.ds(at, 256), :].T

    if picks:
        pltpu.make_async_copy(total, total, total_sem).wait()
    copies = []
    for q in range(QUAD):
        lanes = pl.ds(q * outputs, outputs)
        part = whole.at[:, lanes]
        pltpu.make_async_copy(part, part, error_sem.at[q]).wait()
        gradient = jnp.dot(turned[...], part[...], preferred_element_type=jnp.float32)
        if picks:
            code[:, lanes] = encode(total[:, lanes] + gradient, inverse_ref[0])
            ready = []
            for m, (to, span) in enumerate(zip(layers, spans)):
                rows = pl.ds(m * block, block) if apart else span
                ready.append((code.at[rows, lanes], to_line[m].at[:, lanes]))
                ready.append((code.at[rows, lanes], to_quad[q].at[span]))
        else:
            total[:, lanes] = gradient
            ready = [(total.at[:, lanes], result.at[:, lanes])]
        for source, target in ready:
            copies.append(pltpu.make_async_copy(source, target, out_sem.at[len(copies)]))
            copies[-1].start()
    for copy in copies:
        copy.wait()


def product(line, n_col, tokens, outputs, slab, picks, inverse, candidates, errors, so_far=(), old=()):
    columns = candidates[0].shape[1]
    block = columns // line
    width = len(picks) * block if picks else columns
    depth = line * len(slab) * tokens
    if picks:
        out_shape = [jax.ShapeDtypeStruct((block, QUAD * outputs), jnp.bfloat16)] * len(picks)
        out_shape += [jax.ShapeDtypeStruct((columns, outputs), jnp.bfloat16)] * QUAD
        more = [pltpu.VMEM((width, QUAD * outputs), jnp.bfloat16)]
    else:
        out_shape = [jax.ShapeDtypeStruct((columns, QUAD * outputs), jnp.float32)]
        more = []
    n_in = 1 + len(candidates) + 1 + len(so_far)
    return pl.pallas_call(
        functools.partial(product_kernel, line, n_col, tokens, outputs, slab, picks, len(old)),
        out_shape=out_shape,
        in_specs=[scalar_spec()] + any_specs(n_in - 1 + len(old)),
        out_specs=any_specs(len(out_shape)),
        scratch_shapes=[
            pltpu.VMEM((depth, width), jnp.bfloat16),
            pltpu.VMEM((width, depth), jnp.bfloat16),
            pltpu.VMEM((depth, QUAD * outputs), jnp.bfloat16),
            pltpu.VMEM((width, QUAD * outputs), jnp.float32),
            *more,
            pltpu.SemaphoreType.DMA((line,)),
            pltpu.SemaphoreType.DMA((QUAD,)),
            *([pltpu.SemaphoreType.DMA] if picks else []),
            pltpu.SemaphoreType.DMA((2 * line * QUAD,)),
        ],
        input_output_aliases={n_in + i: len(picks) + i for i in range(len(old))},
        compiler_params=pltpu.CompilerParams(vmem_limit_bytes=56 * 2**20),
        cost_estimate=pl.CostEstimate(flops=2 * width * depth * QUAD * outputs, bytes_accessed=0, transcendentals=0),
        name="product",
    )(inverse, *candidates, errors, *so_far, *old)


def weight_kernel(line, scale_ref, *refs):
    pieces, refs = refs[:QUAD], refs[QUAD:]
    master, one, two = refs[:3]
    outs, (held, sem) = refs[3:7], refs[7:]
    _, quarter, _ = my_place()

    @pl.when(pl.program_id(0) == 0)
    def _():
        copies = []
        for d, piece in enumerate(pieces):
            rows = piece.shape[0] // line
            for h in range(line):
                source, target = piece.at[pl.ds(h * rows, rows)], held.at[h, quarter ^ d]
                copies.append(pltpu.make_async_copy(source, target, sem.at[len(copies)]))
        for copy in copies:
            copy.start()
        for copy in copies:
            copy.wait()

    code = held[pl.program_id(0)]
    gradient = decode(code.reshape(code.shape[0] * code.shape[1], code.shape[2]), scale_ref[0]).T
    for out, value in zip(outs, adam_update(master[...], one[...], two[...], gradient)):
        out[...] = value


def weight_update(line, scale, pieces, master, one, two):
    outputs, columns = master.shape
    tile = pl.BlockSpec((outputs, columns // line), lambda h: (0, h))
    return pl.pallas_call(
        functools.partial(weight_kernel, line),
        grid=(line,),
        out_shape=[
            jax.ShapeDtypeStruct(master.shape, t) for t in (jnp.float32, jnp.bfloat16, jnp.bfloat16, jnp.bfloat16)
        ],
        in_specs=[scalar_spec()] + any_specs(len(pieces)) + [tile] * 3,
        out_specs=[tile] * 4,
        scratch_shapes=[
            pltpu.VMEM((line, QUAD, columns // line // QUAD, outputs), jnp.bfloat16),
            pltpu.SemaphoreType.DMA((QUAD * line,)),
        ],
        compiler_params=pltpu.CompilerParams(vmem_limit_bytes=56 * 2**20),
        cost_estimate=BRIEF,
        name="weight_update",
    )(scale, *pieces, master, one, two)


def feedback_kernel(line, odd, n_held, _, scale_ref, *refs):
    pieces, refs = refs[: line // 2], refs[line // 2 :]
    (master, one, two), refs = refs[:3], refs[3 + n_held :]
    outs, (held, sem) = refs[:4], refs[4:]
    layer, quarter, _ = my_place()
    outputs = held.shape[-1]

    @pl.when((pl.program_id(0) == 0) & (pl.program_id(1) == 0))
    def _():
        copies = []
        for i, piece in enumerate(pieces):
            half = (layer ^ (2 * i + odd)) // 2
            for d in range(QUAD):
                source, target = piece.at[:, pl.ds(d * outputs, outputs)], held.at[half, quarter ^ d]
                copies.append(pltpu.make_async_copy(source, target, sem.at[len(copies)]))
        for copy in copies:
            copy.start()
        for copy in copies:
            copy.wait()

    rows = master.shape[1]
    at = pl.ds(pl.multiple_of(pl.program_id(1) * rows, 16), rows)
    for q in range(QUAD):
        lanes = pl.ds(q * outputs, outputs)
        gradient = decode(held[pl.program_id(0), q, at, :], scale_ref[0])
        values = adam_update(master[0, :, lanes], one[0, :, lanes], two[0, :, lanes], gradient)
        for out, value in zip(outs, values):
            out[0, :, lanes] = value


def feedback_update(line, share, odd, scale, pieces, master, one, two, held):
    block, width = master.shape[1], master.shape[2] // share
    rows = 64 if block % 64 == 0 else block

    def place(i, t, first):
        group, s = unslot(2 * i + first[0], share)
        return group, t, s

    tile = pl.BlockSpec((1, rows, width), place)
    first = ((my_place()[0] ^ odd) % 2)[None].astype(jnp.int32)
    return pl.pallas_call(
        functools.partial(feedback_kernel, line, odd, len(held)),
        grid_spec=pltpu.PrefetchScalarGridSpec(
            num_scalar_prefetch=1,
            grid=(line // 2, block // rows),
            in_specs=[scalar_spec()] + any_specs(line // 2) + [tile] * 3 + any_specs(len(held)),
            out_specs=[tile] * 4,
            scratch_shapes=[
                pltpu.VMEM((line // 2, QUAD, block, width // QUAD), jnp.bfloat16),
                pltpu.SemaphoreType.DMA((line // 2 * QUAD,)),
            ],
        ),
        out_shape=[
            jax.ShapeDtypeStruct(master.shape, t) for t in (jnp.float32, jnp.bfloat16, jnp.bfloat16, jnp.bfloat16)
        ],
        input_output_aliases={2 + line // 2 + 3 + i: i for i in range(len(held))},
        compiler_params=pltpu.CompilerParams(vmem_limit_bytes=56 * 2**20),
        cost_estimate=BRIEF,
        name="feedback_update",
    )(first, scale, *pieces, master, one, two, *held)


def make(n_row, n_col):
    line = n_row // QUAD
    share = line // n_col

    def permute(x, move):
        pairs = []
        for r in range(n_row):
            for c in range(n_col):
                to = move(r // QUAD, r % QUAD, c)
                if to is not None:
                    pairs.append((r * n_col + c, (to[0] * QUAD + to[1]) * n_col + to[2]))
        return lax.ppermute(x, ("row", "col"), pairs)

    def along_quad(x, d):
        return permute(x, lambda h, q, c: (h, q ^ d, c))

    def along_col(x, d):
        return permute(x, lambda h, q, c: (h, q, c ^ d))

    def up(x, k):
        return permute(x, lambda h, q, c: (h + 1, q, c) if k <= h < line - 1 else None)

    def down(x, k):
        return permute(x, lambda h, q, c: (h - 1, q, c) if 0 < h < line - k else None)

    layers = [
        [(h * QUAD + q) * n_col + c for c in range(n_col) for q in range(QUAD)] for h in range(line)
    ]

    def shards(
        errors,
        inputs,
        weight,
        weight_moment_one,
        weight_moment_two,
        feedback,
        feedback_moment_one,
        feedback_moment_two,
    ):
        layer, quarter, column = my_place()
        tokens = inputs.shape[0]
        block = inputs.shape[1] // n_row
        outputs = errors.shape[1]

        squares = longest(errors, inputs)
        of_errors = lax.broadcasted_iota(jnp.int32, squares.shape, 0) < 4

        def combine(mine, others, same_tokens):
            for other in others:
                mine = jnp.where(of_errors == same_tokens, jnp.maximum(mine, other), mine + other)
            return mine

        squares_of_line = combine(
            squares,
            [permute(squares, lambda h, q, c: (h ^ d, q, c)) for d in range(1, line)],
            True,
        )
        squares = squares_of_line
        for d in (1, 2):
            squares = combine(squares, [along_quad(squares, d)], True)
        for bit in range((n_col - 1).bit_length()):
            squares = combine(squares, [along_col(squares, 1 << bit)], False)
        lengths = jnp.sqrt(jnp.stack([squares[0, 0], squares[4, 0]])) * 2.0**-40
        bound = lengths[0] * lengths[1] * 1.01
        bound = jnp.where(bound > 0.0, bound, 1.0)
        inverse, scale = (2.0**HEAD / bound)[None], (bound * 2.0**-HEAD)[None]

        if block % 128 == 0:
            own = pack(line, inputs)
        else:
            columns = inputs.reshape(tokens, line, QUAD, block)
            own = [
                lax.dynamic_index_in_dim(columns, quarter ^ d, 2, keepdims=False).reshape(tokens, line * block)
                for d in range(QUAD)
            ]
        own = [own[0]] + [along_quad(own[d], d) for d in range(1, QUAD)]

        def along_line(start):
            ups, downs = [start], [start]
            for k in range(line - 1):
                ups.append(up(ups[-1], k))
                downs.append(down(downs[-1], k))
            return ups[:0:-1] + downs

        near = along_line(jnp.concatenate([own[0], after(own[1], squares_of_line)], axis=0))
        start = jnp.concatenate([after(own[2], near[line - 2], near[line]), own[3]], axis=0)
        far = along_line(start)
        whole_errors = lax.all_gather(
            after(errors, start), ("row", "col"), axis=0, tiled=True, axis_index_groups=layers
        )
        so_far = product(line, n_col, tokens, outputs, (0, 1), (), inverse, near, whole_errors)
        even, odd = tuple(range(0, line, 2)), tuple(range(1, line, 2))
        for_feedback, for_weight = {}, ()
        for picks in (even, odd) if block % 128 == 0 else (even + odd,):
            codes = product(
                line, n_col, tokens, outputs, (2, 3), picks, inverse, far, whole_errors, so_far, for_weight
            )
            for j, code in zip(picks, codes):
                if j % 2:
                    code = after(code, for_feedback[j - 1])
                for_feedback[j] = permute(code, lambda h, q, c: (slot(h, c, share) ^ j, q, h // share))
            for_weight = codes[len(picks) :]
        for_weight = [along_quad(code, d) if d else code for d, code in enumerate(for_weight)]

        def update_feedback(odd, held, *others):
            return feedback_update(
                line,
                share,
                odd,
                after(scale, *others),
                [for_feedback[j] for j in range(odd, line, 2)],
                feedback,
                feedback_moment_one,
                feedback_moment_two,
                held,
            )

        new_feedback = update_feedback(0, [])
        new_weight = weight_update(
            line, after(scale, new_feedback[1]), for_weight, weight, weight_moment_one, weight_moment_two
        )
        new_feedback = update_feedback(1, new_feedback, new_weight[1])
        return (*new_weight, *new_feedback)

    return shards


def solution(mesh):
    forward, backward = P("row", "col"), P(None, "row", "col")
    return jax.shard_map(
        make(mesh.shape["row"], mesh.shape["col"]),
        mesh=mesh,
        in_specs=(P("col", "row"), forward, forward, forward, forward, backward, backward, backward),
        out_specs=(forward,) * 4 + (backward,) * 4,
        check_vma=False,
    )
```

```python
import functools
import math

import jax
import jax.numpy as jnp
from jax import lax
from jax.experimental import pallas as pl
from jax.experimental.pallas import tpu as pltpu
from jax.sharding import PartitionSpec as P

beta_one = 0.9
beta_two = 0.999
learn_rate = 0.02
decay_rate = 0.1
epsilon = 1e-08
bias_one = 1.0
bias_two = 0.63230458

POWER = 13
HEAD = 9.7

BRIEF = pl.CostEstimate(flops=0, bytes_accessed=0, transcendentals=0)

QUAD = 4


def adam_update(master, moment_one, moment_two, gradient):
    first_new = beta_one * moment_one.astype(jnp.float32) + (1.0 - beta_one) * gradient
    second_new = beta_two * moment_two.astype(jnp.float32) + (1.0 - beta_two) * gradient * gradient
    corrected = second_new * (1.0 / bias_two)
    divisor = corrected * lax.rsqrt(corrected) + epsilon
    inverse = pl.reciprocal(divisor, approx=True)
    inverse = inverse * (2.0 - divisor * inverse)
    master_new = master * (1.0 - learn_rate * decay_rate) - (learn_rate / bias_one) * first_new * inverse
    return (
        master_new,
        first_new.astype(jnp.bfloat16),
        second_new.astype(jnp.bfloat16),
        master_new.astype(jnp.bfloat16),
    )


def encode(gradient, inverse):
    u = gradient * inverse
    u2 = u * u
    u4 = u2 * u2
    return (u4 * u4 * u4 * u).astype(jnp.bfloat16)


def decode(code, scale):
    y = code.astype(jnp.float32)
    size = jnp.exp2(jnp.log(jnp.abs(y)) * (1.0 / (POWER * math.log(2.0)))) * scale
    return jnp.where(y < 0.0, -size, size)


def slot(layer, column, share):
    return column * share + (layer + column) % share


def unslot(index, share):
    return index // share, (index + index // share * (share - 1)) % share


def my_place():
    row = lax.axis_index("row")
    return row // QUAD, row % QUAD, lax.axis_index("col")


def scalar_spec():
    return pl.BlockSpec(memory_space=pltpu.SMEM)


def any_specs(n):
    return [pl.BlockSpec(memory_space=pl.ANY)] * n


def after(value, *others):
    return lax.optimization_barrier((value, *others))[0]


def pack_kernel(line, x_ref, *outs):
    _, quarter, _ = my_place()
    block = x_ref.shape[1] // (line * QUAD)
    for d, out in enumerate(outs):
        for h in range(line):
            start = pl.multiple_of((h * QUAD + (quarter ^ d)) * block, block)
            out[:, pl.ds(h * block, block)] = x_ref[:, pl.ds(start, block)]


def pack(line, x):
    return pl.pallas_call(
        functools.partial(pack_kernel, line),
        out_shape=[jax.ShapeDtypeStruct((x.shape[0], x.shape[1] // QUAD), x.dtype)] * QUAD,
        in_specs=[pl.BlockSpec(memory_space=pltpu.VMEM)],
        out_specs=[pl.BlockSpec(memory_space=pltpu.VMEM)] * QUAD,
        compiler_params=pltpu.CompilerParams(vmem_limit_bytes=32 * 2**20),
        cost_estimate=BRIEF,
        name="pack",
    )(x)


def longest_kernel(errors_ref, inputs_ref, out_ref):
    for half, ref in enumerate((errors_ref, inputs_ref)):
        total = jnp.zeros((1, ref.shape[1]), jnp.float32)
        step = min(256, ref.shape[0])
        for start in range(0, ref.shape[0], step):
            x = ref[pl.ds(start, step), :].astype(jnp.float32) * 2.0**40
            total = total + jnp.sum(x * x, axis=0, keepdims=True)
        out_ref[pl.ds(half * 4, 4), :] = jnp.broadcast_to(jnp.max(total, axis=1, keepdims=True), (4, 128))


def longest(errors, inputs):
    return pl.pallas_call(
        longest_kernel,
        out_shape=jax.ShapeDtypeStruct((8, 128), jnp.float32),
        in_specs=[pl.BlockSpec(memory_space=pltpu.VMEM)] * 2,
        out_specs=pl.BlockSpec(memory_space=pltpu.VMEM),
        compiler_params=pltpu.CompilerParams(vmem_limit_bytes=32 * 2**20),
        cost_estimate=BRIEF,
        name="longest",
    )(errors, inputs)


def product_kernel(line, n_col, tokens, outputs, slab, picks, n_old, *refs):
    share = line // n_col
    if picks:
        inverse_ref, refs = refs[0], refs[1:]
    candidates, refs = refs[: 2 * line - 1], refs[2 * line - 1 :]
    errors, refs = refs[0], refs[1:]
    layer, quarter, column = my_place()
    depth = len(slab) * tokens
    block = candidates[0].shape[1] // line
    if picks:
        so_far, refs = refs[0], refs[1 + n_old :]
        to_line, to_quad, refs = refs[: len(picks)], refs[len(picks) : len(picks) + QUAD], refs[len(picks) + QUAD :]
        held, turned, whole, total, code, in_sem, error_sem, total_sem, out_sem = refs
    else:
        result, held, turned, whole, total, in_sem, error_sem, out_sem = refs
    apart = picks and len(picks) < line
    layers = [slot(layer, column, share) ^ j for j in picks or ()]
    spans = [pl.ds(pl.multiple_of(to * block, block), block) for to in layers]

    for n in range(line):
        source = (column ^ (n // share)) * share + n % share
        for i, candidate in enumerate(candidates):

            @pl.when(source - layer == i - (line - 1))
            def _():
                rows = pl.ds(n * depth, depth)
                if apart:
                    for m, span in enumerate(spans):
                        part = held.at[rows, pl.ds(m * block, block)]
                        pltpu.make_async_copy(candidate.at[:, span], part, in_sem.at[n]).start()
                else:
                    pltpu.make_async_copy(candidate, held.at[rows], in_sem.at[n]).start()

    for q in range(QUAD):
        for n in range(line):
            for m, d in enumerate(slab):
                start = (column ^ (n // share)) * QUAD + (quarter ^ q)
                start = ((start * share + n % share) * QUAD + (quarter ^ d)) * tokens
                pltpu.make_async_copy(
                    errors.at[pl.ds(pl.multiple_of(start, tokens), tokens)],
                    whole.at[pl.ds(n * depth + m * tokens, tokens), pl.ds(q * outputs, outputs)],
                    error_sem.at[q],
                ).start()
    if apart:
        for m, span in enumerate(spans):
            pltpu.make_async_copy(so_far.at[span], total.at[pl.ds(m * block, block)], total_sem).start()
    elif picks:
        pltpu.make_async_copy(so_far, total, total_sem).start()

    for n in range(line):
        part = held.at[pl.ds(n * depth, depth)]
        pltpu.make_async_copy(part, part, in_sem.at[n]).wait()

        @pl.loop(n * depth // 256, (n + 1) * depth // 256)
        def _(i):
            at = pl.multiple_of(i * 256, 256)
            turned[:, pl.ds(at, 256)] = held[pl.ds(at, 256), :].T

    if picks:
        pltpu.make_async_copy(total, total, total_sem).wait()
    copies = []
    for q in range(QUAD):
        lanes = pl.ds(q * outputs, outputs)
        part = whole.at[:, lanes]
        pltpu.make_async_copy(part, part, error_sem.at[q]).wait()
        gradient = jnp.dot(turned[...], part[...], preferred_element_type=jnp.float32)
        if picks:
            code[:, lanes] = encode(total[:, lanes] + gradient, inverse_ref[0])
            ready = []
            for m, (to, span) in enumerate(zip(layers, spans)):
                rows = pl.ds(m * block, block) if apart else span
                ready.append((code.at[rows, lanes], to_line[m].at[:, lanes]))
                ready.append((code.at[rows, lanes], to_quad[q].at[span]))
        else:
            total[:, lanes] = gradient
            ready = [(total.at[:, lanes], result.at[:, lanes])]
        for source, target in ready:
            copies.append(pltpu.make_async_copy(source, target, out_sem.at[len(copies)]))
            copies[-1].start()
    for copy in copies:
        copy.wait()


def product(line, n_col, tokens, outputs, slab, picks, inverse, candidates, errors, so_far=(), old=()):
    columns = candidates[0].shape[1]
    block = columns // line
    width = len(picks) * block if picks else columns
    depth = line * len(slab) * tokens
    if picks:
        out_shape = [jax.ShapeDtypeStruct((block, QUAD * outputs), jnp.bfloat16)] * len(picks)
        out_shape += [jax.ShapeDtypeStruct((columns, outputs), jnp.bfloat16)] * QUAD
        more = [pltpu.VMEM((width, QUAD * outputs), jnp.bfloat16)]
    else:
        out_shape = [jax.ShapeDtypeStruct((columns, QUAD * outputs), jnp.float32)]
        more = []
    scalars = [inverse] if picks else []
    n_in = len(scalars) + len(candidates) + 1 + len(so_far)
    return pl.pallas_call(
        functools.partial(product_kernel, line, n_col, tokens, outputs, slab, picks, len(old)),
        out_shape=out_shape,
        in_specs=[scalar_spec()] * len(scalars) + any_specs(n_in - len(scalars) + len(old)),
        out_specs=any_specs(len(out_shape)),
        scratch_shapes=[
            pltpu.VMEM((depth, width), jnp.bfloat16),
            pltpu.VMEM((width, depth), jnp.bfloat16),
            pltpu.VMEM((depth, QUAD * outputs), jnp.bfloat16),
            pltpu.VMEM((width, QUAD * outputs), jnp.float32),
            *more,
            pltpu.SemaphoreType.DMA((line,)),
            pltpu.SemaphoreType.DMA((QUAD,)),
            *([pltpu.SemaphoreType.DMA] if picks else []),
            pltpu.SemaphoreType.DMA((2 * line * QUAD,)),
        ],
        input_output_aliases={n_in + i: len(picks) + i for i in range(len(old))},
        compiler_params=pltpu.CompilerParams(vmem_limit_bytes=56 * 2**20),
        cost_estimate=pl.CostEstimate(flops=2 * width * depth * QUAD * outputs, bytes_accessed=0, transcendentals=0),
        name="product",
    )(*scalars, *candidates, errors, *so_far, *old)


def weight_kernel(line, scale_ref, *refs):
    pieces, refs = refs[:QUAD], refs[QUAD:]
    master, one, two = refs[:3]
    outs, (held, sem) = refs[3:7], refs[7:]
    _, quarter, _ = my_place()

    @pl.when(pl.program_id(0) == 0)
    def _():
        copies = []
        for d, piece in enumerate(pieces):
            rows = piece.shape[0] // line
            for h in range(line):
                source, target = piece.at[pl.ds(h * rows, rows)], held.at[h, quarter ^ d]
                copies.append(pltpu.make_async_copy(source, target, sem.at[len(copies)]))
        for copy in copies:
            copy.start()
        for copy in copies:
            copy.wait()

    code = held[pl.program_id(0)]
    gradient = decode(code.reshape(code.shape[0] * code.shape[1], code.shape[2]), scale_ref[0]).T
    for out, value in zip(outs, adam_update(master[...], one[...], two[...], gradient)):
        out[...] = value


def weight_update(line, scale, pieces, master, one, two):
    outputs, columns = master.shape
    tile = pl.BlockSpec((outputs, columns // line), lambda h: (0, h))
    return pl.pallas_call(
        functools.partial(weight_kernel, line),
        grid=(line,),
        out_shape=[
            jax.ShapeDtypeStruct(master.shape, t) for t in (jnp.float32, jnp.bfloat16, jnp.bfloat16, jnp.bfloat16)
        ],
        in_specs=[scalar_spec()] + any_specs(len(pieces)) + [tile] * 3,
        out_specs=[tile] * 4,
        scratch_shapes=[
            pltpu.VMEM((line, QUAD, columns // line // QUAD, outputs), jnp.bfloat16),
            pltpu.SemaphoreType.DMA((QUAD * line,)),
        ],
        compiler_params=pltpu.CompilerParams(vmem_limit_bytes=56 * 2**20),
        cost_estimate=BRIEF,
        name="weight_update",
    )(scale, *pieces, master, one, two)


def feedback_kernel(line, odd, n_held, _, scale_ref, *refs):
    pieces, refs = refs[: line // 2], refs[line // 2 :]
    (master, one, two), refs = refs[:3], refs[3 + n_held :]
    outs, (held, sem) = refs[:4], refs[4:]
    layer, quarter, _ = my_place()
    outputs = held.shape[-1]

    @pl.when((pl.program_id(0) == 0) & (pl.program_id(1) == 0))
    def _():
        copies = []
        for i, piece in enumerate(pieces):
            half = (layer ^ (2 * i + odd)) // 2
            for d in range(QUAD):
                source, target = piece.at[:, pl.ds(d * outputs, outputs)], held.at[half, quarter ^ d]
                copies.append(pltpu.make_async_copy(source, target, sem.at[len(copies)]))
        for copy in copies:
            copy.start()
        for copy in copies:
            copy.wait()

    rows = master.shape[1]
    at = pl.ds(pl.multiple_of(pl.program_id(1) * rows, 16), rows)
    for q in range(QUAD):
        lanes = pl.ds(q * outputs, outputs)
        gradient = decode(held[pl.program_id(0), q, at, :], scale_ref[0])
        values = adam_update(master[0, :, lanes], one[0, :, lanes], two[0, :, lanes], gradient)
        for out, value in zip(outs, values):
            out[0, :, lanes] = value


def feedback_update(line, share, odd, scale, pieces, master, one, two, held):
    block, width = master.shape[1], master.shape[2] // share
    rows = 128 if block % 128 == 0 else block

    def place(i, t, first):
        group, s = unslot(2 * i + first[0], share)
        return group, t, s

    tile = pl.BlockSpec((1, rows, width), place)
    first = ((my_place()[0] ^ odd) % 2)[None].astype(jnp.int32)
    return pl.pallas_call(
        functools.partial(feedback_kernel, line, odd, len(held)),
        grid_spec=pltpu.PrefetchScalarGridSpec(
            num_scalar_prefetch=1,
            grid=(line // 2, block // rows),
            in_specs=[scalar_spec()] + any_specs(line // 2) + [tile] * 3 + any_specs(len(held)),
            out_specs=[tile] * 4,
            scratch_shapes=[
                pltpu.VMEM((line // 2, QUAD, block, width // QUAD), jnp.bfloat16),
                pltpu.SemaphoreType.DMA((line // 2 * QUAD,)),
            ],
        ),
        out_shape=[
            jax.ShapeDtypeStruct(master.shape, t) for t in (jnp.float32, jnp.bfloat16, jnp.bfloat16, jnp.bfloat16)
        ],
        input_output_aliases={2 + line // 2 + 3 + i: i for i in range(len(held))},
        compiler_params=pltpu.CompilerParams(vmem_limit_bytes=56 * 2**20),
        cost_estimate=BRIEF,
        name="feedback_update",
    )(first, scale, *pieces, master, one, two, *held)


def make(n_row, n_col):
    line = n_row // QUAD
    share = line // n_col

    def permute(x, move):
        pairs = []
        for r in range(n_row):
            for c in range(n_col):
                to = move(r // QUAD, r % QUAD, c)
                if to is not None:
                    pairs.append((r * n_col + c, (to[0] * QUAD + to[1]) * n_col + to[2]))
        return lax.ppermute(x, ("row", "col"), pairs)

    def along_quad(x, d):
        return permute(x, lambda h, q, c: (h, q ^ d, c))

    def along_col(x, d):
        return permute(x, lambda h, q, c: (h, q, c ^ d))

    def up(x, k):
        return permute(x, lambda h, q, c: (h + 1, q, c) if k <= h < line - 1 else None)

    def down(x, k):
        return permute(x, lambda h, q, c: (h - 1, q, c) if 0 < h < line - k else None)

    layers = [
        [(h * QUAD + q) * n_col + c for c in range(n_col) for q in range(QUAD)] for h in range(line)
    ]

    def shards(
        errors,
        inputs,
        weight,
        weight_moment_one,
        weight_moment_two,
        feedback,
        feedback_moment_one,
        feedback_moment_two,
    ):
        layer, quarter, column = my_place()
        tokens = inputs.shape[0]
        block = inputs.shape[1] // n_row
        outputs = errors.shape[1]

        if block % 128 == 0:
            own = pack(line, inputs)
        else:
            columns = inputs.reshape(tokens, line, QUAD, block)
            own = [
                lax.dynamic_index_in_dim(columns, quarter ^ d, 2, keepdims=False).reshape(tokens, line * block)
                for d in range(QUAD)
            ]
        own = [own[0]] + [along_quad(own[d], d) for d in range(1, QUAD)]

        def along_line(start):
            ups, downs = [start], [start]
            for k in range(line - 1):
                ups.append(up(ups[-1], k))
                downs.append(down(downs[-1], k))
            return ups[:0:-1] + downs

        near = along_line(jnp.concatenate(own[:2], axis=0))

        squares = after(longest(errors, inputs), near[line - 2], near[line])
        of_errors = lax.broadcasted_iota(jnp.int32, squares.shape, 0) < 4

        def combine(mine, others, same_tokens):
            for other in others:
                mine = jnp.where(of_errors == same_tokens, jnp.maximum(mine, other), mine + other)
            return mine

        for bit in range((n_col - 1).bit_length()):
            squares = combine(squares, [along_col(squares, 1 << bit)], False)
        start = jnp.concatenate([after(own[2], squares), own[3]], axis=0)
        far = along_line(start)
        for d in (1, 2):
            squares = combine(squares, [along_quad(squares, d)], True)
        squares = after(squares, near[0], near[-1])
        others = [permute(squares, lambda h, q, c: (h ^ d, q, c)) for d in range(1, line)]
        squares = combine(squares, others, True)
        lengths = jnp.sqrt(jnp.stack([squares[0, 0], squares[4, 0]])) * 2.0**-40
        bound = lengths[0] * lengths[1] * 1.01
        bound = jnp.where(bound > 0.0, bound, 1.0)
        inverse, scale = (2.0**HEAD / bound)[None], (bound * 2.0**-HEAD)[None]
        whole_errors = lax.all_gather(
            after(errors, start), ("row", "col"), axis=0, tiled=True, axis_index_groups=layers
        )
        so_far = product(line, n_col, tokens, outputs, (0, 1), (), None, near, whole_errors)
        even, odd = tuple(range(0, line, 2)), tuple(range(1, line, 2))
        for_feedback, for_weight = {}, ()
        for picks in (even, odd) if block % 128 == 0 else (even + odd,):
            codes = product(
                line, n_col, tokens, outputs, (2, 3), picks, inverse, far, whole_errors, so_far, for_weight
            )
            for j, code in zip(picks, codes):
                if j % 2:
                    code = after(code, for_feedback[j - 1])
                for_feedback[j] = permute(code, lambda h, q, c: (slot(h, c, share) ^ j, q, h // share))
            for_weight = codes[len(picks) :]
        for_weight = [along_quad(code, d) if d else code for d, code in enumerate(for_weight)]

        def update_feedback(odd, held, *others):
            return feedback_update(
                line,
                share,
                odd,
                after(scale, *others),
                [for_feedback[j] for j in range(odd, line, 2)],
                feedback,
                feedback_moment_one,
                feedback_moment_two,
                held,
            )

        new_feedback = update_feedback(0, [])
        new_weight = weight_update(
            line, after(scale, new_feedback[1]), for_weight, weight, weight_moment_one, weight_moment_two
        )
        new_feedback = update_feedback(1, new_feedback, new_weight[1])
        return (*new_weight, *new_feedback)

    return shards


def solution(mesh):
    forward, backward = P("row", "col"), P(None, "row", "col")
    return jax.shard_map(
        make(mesh.shape["row"], mesh.shape["col"]),
        mesh=mesh,
        in_specs=(P("col", "row"), forward, forward, forward, forward, backward, backward, backward),
        out_specs=(forward,) * 4 + (backward,) * 4,
        check_vma=False,
    )
```

```python
import functools
import math

import jax
import jax.numpy as jnp
from jax import lax
from jax.experimental import pallas as pl
from jax.experimental.pallas import tpu as pltpu
from jax.sharding import PartitionSpec as P

beta_one = 0.9
beta_two = 0.999
learn_rate = 0.02
decay_rate = 0.1
epsilon = 1e-08
bias_one = 1.0
bias_two = 0.63230458

POWER = 13
HEAD = 9.7

BRIEF = pl.CostEstimate(flops=0, bytes_accessed=0, transcendentals=0)

QUAD = 4


def adam_update(master, moment_one, moment_two, gradient):
    first_new = beta_one * moment_one.astype(jnp.float32) + (1.0 - beta_one) * gradient
    second_new = beta_two * moment_two.astype(jnp.float32) + (1.0 - beta_two) * gradient * gradient
    corrected = second_new * (1.0 / bias_two)
    divisor = corrected * lax.rsqrt(corrected) + epsilon
    inverse = pl.reciprocal(divisor, approx=True)
    inverse = inverse * (2.0 - divisor * inverse)
    master_new = master * (1.0 - learn_rate * decay_rate) - (learn_rate / bias_one) * first_new * inverse
    return (
        master_new,
        first_new.astype(jnp.bfloat16),
        second_new.astype(jnp.bfloat16),
        master_new.astype(jnp.bfloat16),
    )


def encode(gradient, inverse):
    u = gradient * inverse
    u2 = u * u
    u4 = u2 * u2
    return (u4 * u4 * u4 * u).astype(jnp.bfloat16)


def decode(code, scale):
    y = code.astype(jnp.float32)
    size = jnp.exp2(jnp.log(jnp.abs(y)) * (1.0 / (POWER * math.log(2.0)))) * scale
    return jnp.where(y < 0.0, -size, size)


def slot(layer, column, share):
    return column * share + (layer + column) % share


def unslot(index, share):
    return index // share, (index + index // share * (share - 1)) % share


def my_place():
    row = lax.axis_index("row")
    return row // QUAD, row % QUAD, lax.axis_index("col")


def scalar_spec():
    return pl.BlockSpec(memory_space=pltpu.SMEM)


def any_specs(n):
    return [pl.BlockSpec(memory_space=pl.ANY)] * n


def after(value, *others):
    return lax.optimization_barrier((value, *others))[0]


def pack_kernel(line, x_ref, *outs):
    _, quarter, _ = my_place()
    block = x_ref.shape[1] // (line * QUAD)
    for d, out in enumerate(outs):
        for h in range(line):
            start = pl.multiple_of((h * QUAD + (quarter ^ d)) * block, block)
            out[:, pl.ds(h * block, block)] = x_ref[:, pl.ds(start, block)]


def pack(line, x):
    return pl.pallas_call(
        functools.partial(pack_kernel, line),
        out_shape=[jax.ShapeDtypeStruct((x.shape[0], x.shape[1] // QUAD), x.dtype)] * QUAD,
        in_specs=[pl.BlockSpec(memory_space=pltpu.VMEM)],
        out_specs=[pl.BlockSpec(memory_space=pltpu.VMEM)] * QUAD,
        compiler_params=pltpu.CompilerParams(vmem_limit_bytes=32 * 2**20),
        cost_estimate=BRIEF,
        name="pack",
    )(x)


def longest_kernel(errors_ref, inputs_ref, out_ref):
    for half, ref in enumerate((errors_ref, inputs_ref)):
        total = jnp.zeros((1, ref.shape[1]), jnp.float32)
        step = min(256, ref.shape[0])
        for start in range(0, ref.shape[0], step):
            x = ref[pl.ds(start, step), :].astype(jnp.float32) * 2.0**40
            total = total + jnp.sum(x * x, axis=0, keepdims=True)
        out_ref[pl.ds(half * 4, 4), :] = jnp.broadcast_to(jnp.max(total, axis=1, keepdims=True), (4, 128))


def longest(errors, inputs):
    return pl.pallas_call(
        longest_kernel,
        out_shape=jax.ShapeDtypeStruct((8, 128), jnp.float32),
        in_specs=[pl.BlockSpec(memory_space=pltpu.VMEM)] * 2,
        out_specs=pl.BlockSpec(memory_space=pltpu.VMEM),
        compiler_params=pltpu.CompilerParams(vmem_limit_bytes=32 * 2**20),
        cost_estimate=BRIEF,
        name="longest",
    )(errors, inputs)


def product_kernel(line, n_col, tokens, outputs, slab, picks, n_old, *refs):
    share = line // n_col
    if picks:
        inverse_ref, refs = refs[0], refs[1:]
    candidates, refs = refs[: 2 * line - 1], refs[2 * line - 1 :]
    errors, refs = refs[0], refs[1:]
    layer, quarter, column = my_place()
    depth = len(slab) * tokens
    block = candidates[0].shape[1] // line
    if picks:
        so_far, refs = refs[0], refs[1 + n_old :]
        to_line, to_quad, refs = refs[: len(picks)], refs[len(picks) : len(picks) + QUAD], refs[len(picks) + QUAD :]
        held, turned, whole, total, code, in_sem, error_sem, total_sem, out_sem = refs
    else:
        result, held, turned, whole, total, in_sem, error_sem, out_sem = refs
    apart = picks and len(picks) < line
    layers = [slot(layer, column, share) ^ j for j in picks or ()]
    spans = [pl.ds(pl.multiple_of(to * block, block), block) for to in layers]

    for n in range(line):
        source = (column ^ (n // share)) * share + n % share
        for i, candidate in enumerate(candidates):

            @pl.when(source - layer == i - (line - 1))
            def _():
                rows = pl.ds(n * depth, depth)
                if apart:
                    for m, span in enumerate(spans):
                        part = held.at[rows, pl.ds(m * block, block)]
                        pltpu.make_async_copy(candidate.at[:, span], part, in_sem.at[n]).start()
                else:
                    pltpu.make_async_copy(candidate, held.at[rows], in_sem.at[n]).start()

    for q in range(QUAD):
        for n in range(line):
            for m, d in enumerate(slab):
                start = (column ^ (n // share)) * QUAD + (quarter ^ q)
                start = ((start * share + n % share) * QUAD + (quarter ^ d)) * tokens
                pltpu.make_async_copy(
                    errors.at[pl.ds(pl.multiple_of(start, tokens), tokens)],
                    whole.at[pl.ds(n * depth + m * tokens, tokens), pl.ds(q * outputs, outputs)],
                    error_sem.at[q],
                ).start()
    if apart:
        for m, span in enumerate(spans):
            pltpu.make_async_copy(so_far.at[span], total.at[pl.ds(m * block, block)], total_sem).start()
    elif picks:
        pltpu.make_async_copy(so_far, total, total_sem).start()

    for n in range(line):
        part = held.at[pl.ds(n * depth, depth)]
        pltpu.make_async_copy(part, part, in_sem.at[n]).wait()

        @pl.loop(n * depth // 256, (n + 1) * depth // 256)
        def _(i):
            at = pl.multiple_of(i * 256, 256)
            turned[:, pl.ds(at, 256)] = held[pl.ds(at, 256), :].T

    if picks:
        pltpu.make_async_copy(total, total, total_sem).wait()
    copies = []
    for q in range(QUAD):
        lanes = pl.ds(q * outputs, outputs)
        part = whole.at[:, lanes]
        pltpu.make_async_copy(part, part, error_sem.at[q]).wait()
        gradient = jnp.dot(turned[...], part[...], preferred_element_type=jnp.float32)
        if picks:
            code[:, lanes] = encode(total[:, lanes] + gradient, inverse_ref[0])
            ready = []
            for m, (to, span) in enumerate(zip(layers, spans)):
                rows = pl.ds(m * block, block) if apart else span
                ready.append((code.at[rows, lanes], to_line[m].at[:, lanes]))
                ready.append((code.at[rows, lanes], to_quad[q].at[span]))
        else:
            total[:, lanes] = gradient
            ready = [(total.at[:, lanes], result.at[:, lanes])]
        for source, target in ready:
            copies.append(pltpu.make_async_copy(source, target, out_sem.at[len(copies)]))
            copies[-1].start()
    for copy in copies:
        copy.wait()


def product(line, n_col, tokens, outputs, slab, picks, inverse, candidates, errors, so_far=(), old=()):
    columns = candidates[0].shape[1]
    block = columns // line
    width = len(picks) * block if picks else columns
    depth = line * len(slab) * tokens
    if picks:
        out_shape = [jax.ShapeDtypeStruct((block, QUAD * outputs), jnp.bfloat16)] * len(picks)
        out_shape += [jax.ShapeDtypeStruct((columns, outputs), jnp.bfloat16)] * QUAD
        more = [pltpu.VMEM((width, QUAD * outputs), jnp.bfloat16)]
    else:
        out_shape = [jax.ShapeDtypeStruct((columns, QUAD * outputs), jnp.float32)]
        more = []
    scalars = [inverse] if picks else []
    n_in = len(scalars) + len(candidates) + 1 + len(so_far)
    return pl.pallas_call(
        functools.partial(product_kernel, line, n_col, tokens, outputs, slab, picks, len(old)),
        out_shape=out_shape,
        in_specs=[scalar_spec()] * len(scalars) + any_specs(n_in - len(scalars) + len(old)),
        out_specs=any_specs(len(out_shape)),
        scratch_shapes=[
            pltpu.VMEM((depth, width), jnp.bfloat16),
            pltpu.VMEM((width, depth), jnp.bfloat16),
            pltpu.VMEM((depth, QUAD * outputs), jnp.bfloat16),
            pltpu.VMEM((width, QUAD * outputs), jnp.float32),
            *more,
            pltpu.SemaphoreType.DMA((line,)),
            pltpu.SemaphoreType.DMA((QUAD,)),
            *([pltpu.SemaphoreType.DMA] if picks else []),
            pltpu.SemaphoreType.DMA((2 * line * QUAD,)),
        ],
        input_output_aliases={n_in + i: len(picks) + i for i in range(len(old))},
        compiler_params=pltpu.CompilerParams(vmem_limit_bytes=56 * 2**20),
        cost_estimate=pl.CostEstimate(
            flops=(2 if picks else 40) * width * depth * QUAD * outputs, bytes_accessed=0, transcendentals=0
        ),
        name="product",
    )(*scalars, *candidates, errors, *so_far, *old)


def weight_kernel(line, scale_ref, *refs):
    pieces, refs = refs[:QUAD], refs[QUAD:]
    master, one, two = refs[:3]
    outs, (held, sem) = refs[3:7], refs[7:]
    _, quarter, _ = my_place()

    @pl.when(pl.program_id(0) == 0)
    def _():
        copies = []
        for d, piece in enumerate(pieces):
            rows = piece.shape[0] // line
            for h in range(line):
                source, target = piece.at[pl.ds(h * rows, rows)], held.at[h, quarter ^ d]
                copies.append(pltpu.make_async_copy(source, target, sem.at[len(copies)]))
        for copy in copies:
            copy.start()
        for copy in copies:
            copy.wait()

    code = held[pl.program_id(0)]
    gradient = decode(code.reshape(code.shape[0] * code.shape[1], code.shape[2]), scale_ref[0]).T
    for out, value in zip(outs, adam_update(master[...], one[...], two[...], gradient)):
        out[...] = value


def weight_update(line, scale, pieces, master, one, two):
    outputs, columns = master.shape
    tile = pl.BlockSpec((outputs, columns // line), lambda h: (0, h))
    return pl.pallas_call(
        functools.partial(weight_kernel, line),
        grid=(line,),
        out_shape=[
            jax.ShapeDtypeStruct(master.shape, t) for t in (jnp.float32, jnp.bfloat16, jnp.bfloat16, jnp.bfloat16)
        ],
        in_specs=[scalar_spec()] + any_specs(len(pieces)) + [tile] * 3,
        out_specs=[tile] * 4,
        scratch_shapes=[
            pltpu.VMEM((line, QUAD, columns // line // QUAD, outputs), jnp.bfloat16),
            pltpu.SemaphoreType.DMA((QUAD * line,)),
        ],
        compiler_params=pltpu.CompilerParams(vmem_limit_bytes=56 * 2**20),
        cost_estimate=BRIEF,
        name="weight_update",
    )(scale, *pieces, master, one, two)


def feedback_kernel(line, odd, n_held, _, scale_ref, *refs):
    pieces, refs = refs[: line // 2], refs[line // 2 :]
    (master, one, two), refs = refs[:3], refs[3 + n_held :]
    outs, (held, sem) = refs[:4], refs[4:]
    layer, quarter, _ = my_place()
    outputs = held.shape[-1]

    @pl.when((pl.program_id(0) == 0) & (pl.program_id(1) == 0))
    def _():
        copies = []
        for i, piece in enumerate(pieces):
            half = (layer ^ (2 * i + odd)) // 2
            for d in range(QUAD):
                source, target = piece.at[:, pl.ds(d * outputs, outputs)], held.at[half, quarter ^ d]
                copies.append(pltpu.make_async_copy(source, target, sem.at[len(copies)]))
        for copy in copies:
            copy.start()
        for copy in copies:
            copy.wait()

    rows = master.shape[1]
    at = pl.ds(pl.multiple_of(pl.program_id(1) * rows, 16), rows)
    for q in range(QUAD):
        lanes = pl.ds(q * outputs, outputs)
        gradient = decode(held[pl.program_id(0), q, at, :], scale_ref[0])
        values = adam_update(master[0, :, lanes], one[0, :, lanes], two[0, :, lanes], gradient)
        for out, value in zip(outs, values):
            out[0, :, lanes] = value


def feedback_update(line, share, odd, scale, pieces, master, one, two, held):
    block, width = master.shape[1], master.shape[2] // share
    rows = 128 if block % 128 == 0 else block

    def place(i, t, first):
        group, s = unslot(2 * i + first[0], share)
        return group, t, s

    tile = pl.BlockSpec((1, rows, width), place)
    first = ((my_place()[0] ^ odd) % 2)[None].astype(jnp.int32)
    return pl.pallas_call(
        functools.partial(feedback_kernel, line, odd, len(held)),
        grid_spec=pltpu.PrefetchScalarGridSpec(
            num_scalar_prefetch=1,
            grid=(line // 2, block // rows),
            in_specs=[scalar_spec()] + any_specs(line // 2) + [tile] * 3 + any_specs(len(held)),
            out_specs=[tile] * 4,
            scratch_shapes=[
                pltpu.VMEM((line // 2, QUAD, block, width // QUAD), jnp.bfloat16),
                pltpu.SemaphoreType.DMA((line // 2 * QUAD,)),
            ],
        ),
        out_shape=[
            jax.ShapeDtypeStruct(master.shape, t) for t in (jnp.float32, jnp.bfloat16, jnp.bfloat16, jnp.bfloat16)
        ],
        input_output_aliases={2 + line // 2 + 3 + i: i for i in range(len(held))},
        compiler_params=pltpu.CompilerParams(vmem_limit_bytes=56 * 2**20),
        cost_estimate=BRIEF,
        name="feedback_update",
    )(first, scale, *pieces, master, one, two, *held)


def make(n_row, n_col):
    line = n_row // QUAD
    share = line // n_col

    def permute(x, move):
        pairs = []
        for r in range(n_row):
            for c in range(n_col):
                to = move(r // QUAD, r % QUAD, c)
                if to is not None:
                    pairs.append((r * n_col + c, (to[0] * QUAD + to[1]) * n_col + to[2]))
        return lax.ppermute(x, ("row", "col"), pairs)

    def along_quad(x, d):
        return permute(x, lambda h, q, c: (h, q ^ d, c))

    def along_col(x, d):
        return permute(x, lambda h, q, c: (h, q, c ^ d))

    def up(x, k):
        return permute(x, lambda h, q, c: (h + 1, q, c) if k <= h < line - 1 else None)

    def down(x, k):
        return permute(x, lambda h, q, c: (h - 1, q, c) if 0 < h < line - k else None)

    layers = [
        [(h * QUAD + q) * n_col + c for c in range(n_col) for q in range(QUAD)] for h in range(line)
    ]

    def shards(
        errors,
        inputs,
        weight,
        weight_moment_one,
        weight_moment_two,
        feedback,
        feedback_moment_one,
        feedback_moment_two,
    ):
        layer, quarter, column = my_place()
        tokens = inputs.shape[0]
        block = inputs.shape[1] // n_row
        outputs = errors.shape[1]

        if block % 128 == 0:
            own = pack(line, inputs)
        else:
            columns = inputs.reshape(tokens, line, QUAD, block)
            own = [
                lax.dynamic_index_in_dim(columns, quarter ^ d, 2, keepdims=False).reshape(tokens, line * block)
                for d in range(QUAD)
            ]
        own = [own[0]] + [along_quad(own[d], d) for d in range(1, QUAD)]

        def along_line(start):
            ups, downs = [start], [start]
            for k in range(line - 1):
                ups.append(up(ups[-1], k))
                downs.append(down(downs[-1], k))
            return ups[:0:-1] + downs

        near = along_line(jnp.concatenate(own[:2], axis=0))

        squares = after(longest(errors, inputs), near[line - 2], near[line])
        of_errors = lax.broadcasted_iota(jnp.int32, squares.shape, 0) < 4

        def combine(mine, others, same_tokens):
            for other in others:
                mine = jnp.where(of_errors == same_tokens, jnp.maximum(mine, other), mine + other)
            return mine

        for bit in range((n_col - 1).bit_length()):
            squares = combine(squares, [along_col(squares, 1 << bit)], False)
        start = jnp.concatenate([after(own[2], squares), own[3]], axis=0)
        far = along_line(start)
        for d in (1, 2):
            squares = combine(squares, [along_quad(squares, d)], True)
        squares = after(squares, near[0], near[-1])
        others = [permute(squares, lambda h, q, c: (h ^ d, q, c)) for d in range(1, line)]
        squares = combine(squares, others, True)
        lengths = jnp.sqrt(jnp.stack([squares[0, 0], squares[4, 0]])) * 2.0**-40
        bound = lengths[0] * lengths[1] * 1.01
        bound = jnp.where(bound > 0.0, bound, 1.0)
        inverse, scale = (2.0**HEAD / bound)[None], (bound * 2.0**-HEAD)[None]
        whole_errors = lax.all_gather(
            after(errors, start), ("row", "col"), axis=0, tiled=True, axis_index_groups=layers
        )
        so_far = product(line, n_col, tokens, outputs, (0, 1), (), None, near, whole_errors)
        even, odd = tuple(range(0, line, 2)), tuple(range(1, line, 2))
        for_feedback, for_weight = {}, ()
        for picks in (even, odd) if block % 128 == 0 else (even + odd,):
            codes = product(
                line, n_col, tokens, outputs, (2, 3), picks, inverse, far, whole_errors, so_far, for_weight
            )
            for j, code in zip(picks, codes):
                if j % 2:
                    code = after(code, for_feedback[j - 1])
                for_feedback[j] = permute(code, lambda h, q, c: (slot(h, c, share) ^ j, q, h // share))
            for_weight = codes[len(picks) :]
        for_weight = [along_quad(code, d) if d else code for d, code in enumerate(for_weight)]

        def update_feedback(odd, held, *others):
            return feedback_update(
                line,
                share,
                odd,
                after(scale, *others),
                [for_feedback[j] for j in range(odd, line, 2)],
                feedback,
                feedback_moment_one,
                feedback_moment_two,
                held,
            )

        new_feedback = update_feedback(0, [])
        new_weight = weight_update(
            line, after(scale, new_feedback[1]), for_weight, weight, weight_moment_one, weight_moment_two
        )
        new_feedback = update_feedback(1, new_feedback, new_weight[1])
        return (*new_weight, *new_feedback)

    return shards


def solution(mesh):
    forward, backward = P("row", "col"), P(None, "row", "col")
    return jax.shard_map(
        make(mesh.shape["row"], mesh.shape["col"]),
        mesh=mesh,
        in_specs=(P("col", "row"), forward, forward, forward, forward, backward, backward, backward),
        out_specs=(forward,) * 4 + (backward,) * 4,
        check_vma=False,
    )
```
